32 devices in a mesh: rep: 2 (over y), fsdp: 4 (over z), dp: 2 (over x), sub: 2 (over core).
Axes of the slice: x: 2, y: 2, z: 4, core: 2. Of those that a mesh axis runs over, the one named last changes fastest.
Arguments:
- features: bfloat16 [1024, 4096], P(('rep', 'dp', 'sub'), 'fsdp'), parts along dimension 0, may hold values from -6 to 6
- values: bfloat16 [64, 64, 4864], P('fsdp'), may hold values from -0.15625 to 0.15625
- col_idx: int32 [64, 76], P('fsdp'), may hold values from 0 to 255, as said below
- cotangent: bfloat16 [1024, 16384], P(('rep', 'dp', 'sub'), 'fsdp'), parts along dimension 0, may hold values from -6 to 6
Outputs:
- projected: bfloat16 [1024, 16384], P(('rep', 'dp', 'sub'), 'fsdp'), parts along dimension 0
- input_grad: bfloat16 [1024, 4096], P(('rep', 'dp', 'sub'), 'fsdp'), parts along dimension 0
- weight_grad: float32 [128, 64, 4864], P(('rep', 'fsdp')), parts along dimension 0
The draws below stay inside these ranges and needn't reach their ends.
There are 2 independent parts, one for each index of `rep`. The reference program is written for one: setup_inputs(seed, part) draws one part's arguments, and reference() takes and returns one part's arrays. A program takes and returns all parts, laid end to end along the dimension named above; an argument that names none is the same for every part. Nothing has to cross between parts.
Inputs may be any that keep to these rules, and one draw needn't show every extreme that they name: `col_idx`: each block row lists exactly 76 distinct block columns in ascending order. At most 48 of one block row's columns fall into one aligned group of 64 block columns; in every draw some group holds exactly 48 columns of every block row.
All inputs are finite; a program needn't handle non-finite values.
Results may differ from the reference program's by a relative error of at most 0.0085.
Values may be sent and summed in bfloat16 or wider, within the bound.
A program may use at most 448 MiB of HBM per device.

```python
import jax
import jax.numpy as jnp
from jax import lax

D = 4096
FF = 16384
BS = 64
TOK_DEV = 128
NBR = 64
NBC = 256
KEEP = 76
TC = 64
PER = 48
TOKENS = 512
N_FSDP = 4
N_DP = 2
N_SUB = 2


def draw_col_idx(key, part):
    key = jax.random.fold_in(key, 11)
    key_base, key_boost, key_star = jax.random.split(key, 3)
    group_count = NBC // TC
    baseline_rating = jax.random.randint(key_base, (NBR, NBC), 0, 4096)
    rating_increment = jax.random.randint(key_boost, (group_count,), 0, 3) * 1024
    favoured_block = jax.random.randint(key_star, (), 0, group_count)
    group_lookup = jnp.arange(NBC, dtype=jnp.int32) // TC
    extra_credit = rating_increment[group_lookup] + jnp.where(group_lookup == favoured_block, 16384, 0)
    block_rating = baseline_rating + extra_credit[None, :]
    grouped = block_rating.reshape(NBR, group_count, TC) * TC + jnp.arange(TC, dtype=jnp.int32)
    order = jnp.argsort(-grouped, axis=-1)
    within = jnp.argsort(order, axis=-1).reshape(NBR, NBC)
    allowed = (within < PER).astype(jnp.int32)
    final = (block_rating + allowed * 65536) * NBC + jnp.arange(NBC, dtype=jnp.int32)[None, :]
    _, picked = lax.top_k(final, KEEP)
    return jnp.sort(picked, axis=-1).astype(jnp.int32)


def levels(own_key, extent, shards, smallest, largest):
    loudness, own = 1.0, jax.random.fold_in(own_key, 6)
    for axis_at, blocks in shards:
        heights = jnp.exp(jax.random.uniform(jax.random.fold_in(own, axis_at), (blocks,), jnp.float32, smallest / len(shards), largest / len(shards)))
        loudness = loudness * jnp.repeat(heights, extent[axis_at] // blocks).reshape([-1 if axis == axis_at else 1 for axis in range(len(extent))])
    return loudness


def scatter_about(key, extent, deviation, most, shards=(), kind=jnp.bfloat16):
    result = jax.random.normal(key, extent, jnp.float32) * deviation
    if len(shards) > 0:
        result = levels(key, extent, shards, -0.22, 0.18) * result
    return jnp.clip(result, min=-most, max=most).astype(kind)


def setup_inputs(seed: int = 0, part: int = 0) -> dict:
    seeds = jax.random.split(jax.random.key(seed), 5)
    part_keys = jax.random.split(jax.random.fold_in(seeds[4], part), 5)
    features = scatter_about(part_keys[0], (TOKENS, D), 1.0, 6.0, ((0, 4), (1, 4)))
    values = scatter_about(seeds[1], (NBR, BS, KEEP * BS), (D * 3 // 10) ** -0.5, 0.15625, ((0, 4),))
    col_idx = draw_col_idx(jax.random.fold_in(seeds[4], 71), part)
    cotangent = scatter_about(part_keys[3], (TOKENS, FF), 1.0, 6.0, ((0, 4), (1, 4)))
    return {"features": features, "values": values, "col_idx": col_idx, "cotangent": cotangent}


def dense_weight(values, col_idx):
    blocks = values.reshape(NBR, BS, KEEP, BS).transpose(0, 2, 1, 3)
    row_ids = jnp.broadcast_to(jnp.arange(NBR, dtype=jnp.int32)[:, None], (NBR, KEEP))
    grid = jnp.zeros((NBR, NBC, BS, BS), values.dtype).at[row_ids, col_idx].set(blocks)
    return grid.transpose(0, 2, 1, 3).reshape(D, FF)

def reference(features, values, col_idx, cotangent):
    weight = dense_weight(values, col_idx)
    projected = jnp.dot(features, weight, preferred_element_type=jnp.float32).astype(jnp.bfloat16)
    tile_width = FF // N_FSDP
    token_total = features.shape[0]

    def tile_step(carry_sum, index):
        start = index * tile_width
        grad_part = lax.dynamic_slice_in_dim(cotangent, start, tile_width, 1)
        weight_part = lax.dynamic_slice_in_dim(weight, start, tile_width, 1)
        term = lax.dot_general(grad_part, weight_part, (((1,), (1,)), ((), ())), preferred_element_type=jnp.float32)
        rounded = lax.optimization_barrier(term.astype(jnp.bfloat16))
        return (carry_sum + rounded.astype(jnp.float32), None)
    input_sum, _ = lax.scan(tile_step, jnp.zeros((token_total, D), jnp.float32), jnp.arange(N_FSDP, dtype=jnp.int32))
    input_grad = input_sum.astype(jnp.bfloat16)
    picker = jnp.broadcast_to(col_idx[:, None, :, None], (NBR, BS, KEEP, BS))

    def group_step(carry_sum, index):
        start = index * TOK_DEV
        rows_part = lax.dynamic_slice_in_dim(features, start, TOK_DEV, 0)
        grad_part = lax.dynamic_slice_in_dim(cotangent, start, TOK_DEV, 0)
        full_grad = lax.dot_general(rows_part, grad_part, (((0,), (0,)), ((), ())), preferred_element_type=jnp.float32)
        picked = jnp.take_along_axis(full_grad.reshape(NBR, BS, NBC, BS), picker, axis=2)
        rounded = lax.optimization_barrier(picked.reshape(NBR, BS, KEEP * BS).astype(jnp.bfloat16))
        return (carry_sum + rounded.astype(jnp.float32), None)
    grad_total, _ = lax.scan(group_step, jnp.zeros((NBR, BS, KEEP * BS), jnp.float32), jnp.arange(N_DP * N_SUB, dtype=jnp.int32))
    weight_grad = grad_total / jnp.sqrt(jnp.float32(TOKENS))
    return (projected, input_grad, weight_grad)
```

```python
import functools

import jax
import jax.numpy as jnp
from jax import lax
from jax.experimental import pallas as pl
from jax.experimental.pallas import tpu as pltpu
from jax.sharding import PartitionSpec as P

BS = 64
NBC = 256
FF = BS * NBC
VMEM = 60 * 1024 * 1024


def expand_kernel(idx, vt_ref, w_ref):
    pair = pl.program_id(0)
    keep = vt_ref.shape[0] // BS
    chunk = 512

    @pl.loop(0, FF // chunk)
    def _(i):
        w_ref[pl.ds(pl.multiple_of(i * chunk, chunk), chunk), :] = jnp.zeros(
            (chunk, 2 * BS), w_ref.dtype
        )

    lane = lax.broadcasted_iota(jnp.int32, (BS, 2 * BS), 1)
    for half in range(2):
        mask = (lane >= BS) if half else (lane < BS)

        @pl.loop(0, keep, unroll=4)
        def _(k):
            place = pl.ds(pl.multiple_of(idx[2 * pair + half, k] * BS, BS), BS)
            block = vt_ref[pl.ds(pl.multiple_of(k * BS, BS), BS), :]
            w_ref[place, :] = jnp.where(mask, block, w_ref[place, :])


def expand(col_idx, values_t):
    depth, rows = values_t.shape
    return pl.pallas_call(
        expand_kernel,
        out_shape=jax.ShapeDtypeStruct((FF, rows), values_t.dtype),
        grid_spec=pltpu.PrefetchScalarGridSpec(
            num_scalar_prefetch=1,
            grid=(rows // (2 * BS),),
            in_specs=[pl.BlockSpec((depth, 2 * BS), lambda i, idx: (0, i))],
            out_specs=pl.BlockSpec((FF, 2 * BS), lambda i, idx: (0, i)),
        ),
        compiler_params=pltpu.CompilerParams(vmem_limit_bytes=VMEM),
        cost_estimate=pl.CostEstimate(
            flops=0, bytes_accessed=2 * rows * (FF + depth), transcendentals=0
        ),
    )(col_idx, values_t)


def project_kernel(x_ref, w_ref, o_ref):
    o_ref[0] = lax.dot_general(
        x_ref[...], w_ref[...], (((1,), (1,)), ((), ())), preferred_element_type=jnp.float32
    ).astype(o_ref.dtype)


def project(features, weight_t, tiles):
    tokens, rows = features.shape
    width = FF // tiles
    cols = min(2048, width)
    per = width // cols
    return pl.pallas_call(
        project_kernel,
        out_shape=jax.ShapeDtypeStruct((tiles, tokens, width), jnp.bfloat16),
        grid=(tiles, per),
        in_specs=[
            pl.BlockSpec((tokens, rows), lambda f, j: (0, 0)),
            pl.BlockSpec((cols, rows), lambda f, j: (f * per + j, 0)),
        ],
        out_specs=pl.BlockSpec((1, tokens, cols), lambda f, j: (f, 0, j)),
        compiler_params=pltpu.CompilerParams(vmem_limit_bytes=VMEM),
        cost_estimate=pl.CostEstimate(
            flops=2 * tokens * rows * FF, bytes_accessed=2 * FF * (rows + tokens), transcendentals=0
        ),
    )(features, weight_t)


def back_kernel(g_ref, w_ref, o_ref, total):
    f, j = pl.program_id(0), pl.program_id(1)
    first = jnp.logical_and(f == 0, j == 0)
    last = jnp.logical_and(f == pl.num_programs(0) - 1, j == pl.num_programs(1) - 1)

    @pl.when(first)
    def _():
        total[...] = jnp.zeros_like(total)

    total[...] += jnp.dot(g_ref[0], w_ref[...], preferred_element_type=jnp.float32)

    @pl.when(last)
    def _():
        o_ref[...] = total[...].astype(o_ref.dtype)


def back(cotangent, weight_t):
    tiles, tokens, width = cotangent.shape
    rows = weight_t.shape[1]
    cols = min(2048, width)
    per = width // cols
    return pl.pallas_call(
        back_kernel,
        out_shape=jax.ShapeDtypeStruct((tokens, rows), jnp.bfloat16),
        grid=(tiles, per),
        in_specs=[
            pl.BlockSpec((1, tokens, cols), lambda f, j: (f, 0, j)),
            pl.BlockSpec((cols, rows), lambda f, j: (f * per + j, 0)),
        ],
        out_specs=pl.BlockSpec((tokens, rows), lambda f, j: (0, 0)),
        scratch_shapes=[pltpu.VMEM((tokens, rows), jnp.float32)],
        compiler_params=pltpu.CompilerParams(vmem_limit_bytes=VMEM),
        cost_estimate=pl.CostEstimate(
            flops=2 * tokens * rows * FF, bytes_accessed=2 * FF * (rows + tokens), transcendentals=0
        ),
    )(cotangent, weight_t)


def grad_kernel(scale, idx, x_ref, g_ref, o_ref, dense):
    groups, _, part, width = g_ref.shape
    block_rows, _, kept = o_ref.shape
    cols = min(512, width)
    per = width // cols
    base = pl.program_id(0) * block_rows

    @pl.loop(0, FF // cols)
    def _(c):
        at = pl.ds(pl.multiple_of((c % per) * cols, cols), cols)
        right = g_ref[:, c // per, :, at].reshape(groups * part, cols)
        dense[:, pl.ds(pl.multiple_of(c * cols, cols), cols)] = (
            jnp.dot(x_ref[...], right, preferred_element_type=jnp.float32) * scale
        )

    lane = lax.broadcasted_iota(jnp.int32, (BS, 2 * BS), 1)
    for i in range(block_rows):
        rows = slice(i * BS, (i + 1) * BS)

        @pl.loop(0, kept // (2 * BS), unroll=2)
        def _(q):
            low, high = idx[base + i, 2 * q], idx[base + i, 2 * q + 1]
            a = dense[rows, pl.ds(pl.multiple_of((low // 2) * (2 * BS), 2 * BS), 2 * BS)]
            b = dense[rows, pl.ds(pl.multiple_of((high // 2) * (2 * BS), 2 * BS), 2 * BS)]
            a = pltpu.roll(a, (low % 2) * BS, 1)
            b = pltpu.roll(b, ((high + 1) % 2) * BS, 1)
            o_ref[i, :, pl.ds(pl.multiple_of(q * 2 * BS, 2 * BS), 2 * BS)] = jnp.where(
                lane < BS, a, b
            )


def weight_gradient(col_idx, features_t, cotangent):
    rows, tokens = features_t.shape
    kept = col_idx.shape[1] * BS
    block_rows = min(4, rows // BS)
    return pl.pallas_call(
        functools.partial(grad_kernel, float(tokens) ** -0.5),
        out_shape=jax.ShapeDtypeStruct((rows // BS, BS, kept), jnp.float32),
        grid_spec=pltpu.PrefetchScalarGridSpec(
            num_scalar_prefetch=1,
            grid=(rows // BS // block_rows,),
            in_specs=[
                pl.BlockSpec((block_rows * BS, tokens), lambda i, idx: (i, 0)),
                pl.BlockSpec(
                    cotangent.shape, lambda i, idx: (0, 0, 0, 0), pipeline_mode=pl.Buffered(1)
                ),
            ],
            out_specs=pl.BlockSpec((block_rows, BS, kept), lambda i, idx: (i, 0, 0)),
            scratch_shapes=[pltpu.VMEM((block_rows * BS, FF), jnp.float32)],
        ),
        compiler_params=pltpu.CompilerParams(vmem_limit_bytes=VMEM),
        cost_estimate=pl.CostEstimate(
            flops=2 * tokens * rows * FF,
            bytes_accessed=2 * tokens * FF + 4 * rows * kept,
            transcendentals=0,
        ),
    )(col_idx, features_t, cotangent)


def body(features, values, col_idx, cotangent):
    tiles = lax.axis_size("fsdp")
    rows = values.shape[0] * BS
    token_cotangent = lax.all_gather(cotangent, "fsdp", axis=0)
    all_cotangent = lax.all_gather(token_cotangent, ("dp", "sub"), axis=0)
    all_features = lax.all_gather(features, ("dp", "sub"), axis=0, tiled=True)
    weight_t = expand(col_idx, values.reshape(rows, -1).T)
    partial = project(features, weight_t, tiles)
    projected = lax.psum_scatter(partial, "fsdp", scatter_dimension=0)
    input_grad = back(token_cotangent, weight_t)
    weight_grad = weight_gradient(col_idx, all_features.T, all_cotangent)
    return (projected, input_grad, weight_grad)


def solution(mesh):
    in_specs = (
        P(("rep", "dp", "sub"), "fsdp"),
        P("fsdp", None, None),
        P("fsdp", None),
        P(("rep", "dp", "sub"), "fsdp"),
    )
    out_specs = (
        P(("rep", "dp", "sub"), "fsdp"),
        P(("rep", "dp", "sub"), "fsdp"),
        P(("rep", "fsdp"), None, None),
    )
    return jax.shard_map(body, mesh=mesh, in_specs=in_specs, out_specs=out_specs, check_vma=False)
```

```python
import functools

import jax
import jax.numpy as jnp
from jax import lax
from jax.experimental import pallas as pl
from jax.experimental.pallas import tpu as pltpu
from jax.sharding import PartitionSpec as P

BS = 64
NBC = 256
FF = BS * NBC
VMEM = 60 * 1024 * 1024


def expand_kernel(idx, vt_ref, w_ref):
    pair = pl.program_id(0)
    keep = vt_ref.shape[0] // BS
    chunk = 512

    @pl.loop(0, FF // chunk)
    def _(i):
        w_ref[pl.ds(pl.multiple_of(i * chunk, chunk), chunk), :] = jnp.zeros(
            (chunk, 2 * BS), w_ref.dtype
        )

    lane = lax.broadcasted_iota(jnp.int32, (BS, 2 * BS), 1)
    for half in range(2):
        mask = (lane >= BS) if half else (lane < BS)

        @pl.loop(0, keep, unroll=4)
        def _(k):
            place = pl.ds(pl.multiple_of(idx[2 * pair + half, k] * BS, BS), BS)
            block = vt_ref[pl.ds(pl.multiple_of(k * BS, BS), BS), :]
            w_ref[place, :] = jnp.where(mask, block, w_ref[place, :])


def expand(col_idx, values_t):
    depth, rows = values_t.shape
    return pl.pallas_call(
        expand_kernel,
        out_shape=jax.ShapeDtypeStruct((FF, rows), values_t.dtype),
        grid_spec=pltpu.PrefetchScalarGridSpec(
            num_scalar_prefetch=1,
            grid=(rows // (2 * BS),),
            in_specs=[pl.BlockSpec((depth, 2 * BS), lambda i, idx: (0, i))],
            out_specs=pl.BlockSpec((FF, 2 * BS), lambda i, idx: (0, i)),
        ),
        compiler_params=pltpu.CompilerParams(vmem_limit_bytes=VMEM),
        cost_estimate=pl.CostEstimate(
            flops=0, bytes_accessed=2 * rows * (FF + depth), transcendentals=0
        ),
    )(col_idx, values_t)


def project_kernel(own, x_ref, w_ref, o_ref):
    o_ref[0] = lax.dot_general(
        x_ref[...], w_ref[...], (((1,), (1,)), ((), ())), preferred_element_type=jnp.float32
    ).astype(o_ref.dtype)


def project(own, features, weight_t, tiles):
    tokens, rows = features.shape
    width = FF // tiles
    cols = min(2048, width)
    per = width // cols
    return pl.pallas_call(
        project_kernel,
        out_shape=jax.ShapeDtypeStruct((tiles, tokens, width), jnp.bfloat16),
        grid_spec=pltpu.PrefetchScalarGridSpec(
            num_scalar_prefetch=1,
            grid=(tiles, per),
            in_specs=[
                pl.BlockSpec((tokens, rows), lambda d, j, own: (0, 0)),
                pl.BlockSpec(
                    (cols, rows), lambda d, j, own: (lax.rem(own[0] + d, tiles) * per + j, 0)
                ),
            ],
            out_specs=pl.BlockSpec((1, tokens, cols), lambda d, j, own: (d, 0, j)),
        ),
        compiler_params=pltpu.CompilerParams(vmem_limit_bytes=VMEM),
        cost_estimate=pl.CostEstimate(
            flops=2 * tokens * rows * FF, bytes_accessed=2 * FF * (rows + tokens), transcendentals=0
        ),
    )(own, features, weight_t)


def back_kernel(parts, *refs):
    w_ref, o_ref, total = refs[parts:]
    f = pl.program_id(0)

    @pl.when(f == 0)
    def _():
        total[...] = jnp.zeros_like(total)

    for h in range(parts):
        cols = refs[h].shape[2]
        total[...] += jnp.dot(
            refs[h][0], w_ref[h * cols : (h + 1) * cols, :], preferred_element_type=jnp.float32
        )

    @pl.when(f == pl.num_programs(0) - 1)
    def _():
        o_ref[...] = total[...].astype(o_ref.dtype)


def back(cotangents, weight_t):
    parts = len(cotangents)
    tiles, tokens, cols = cotangents[0].shape
    rows = weight_t.shape[1]
    return pl.pallas_call(
        functools.partial(back_kernel, parts),
        out_shape=jax.ShapeDtypeStruct((tokens, rows), jnp.bfloat16),
        grid=(tiles,),
        in_specs=[pl.BlockSpec((1, tokens, cols), lambda f: (f, 0, 0))] * parts
        + [pl.BlockSpec((parts * cols, rows), lambda f: (f, 0))],
        out_specs=pl.BlockSpec((tokens, rows), lambda f: (0, 0)),
        scratch_shapes=[pltpu.VMEM((tokens, rows), jnp.float32)],
        compiler_params=pltpu.CompilerParams(vmem_limit_bytes=VMEM),
        cost_estimate=pl.CostEstimate(
            flops=2 * tokens * rows * FF, bytes_accessed=2 * FF * (rows + tokens), transcendentals=0
        ),
    )(*cotangents, weight_t)


def grad_kernel(scale, parts, idx, x_ref, *refs):
    o_ref, dense = refs[-2:]
    pieces = refs[:-2]
    groups = len(pieces) // parts
    tiles, part, width = pieces[0].shape
    block_rows, _, kept = o_ref.shape
    cols = min(512, width)
    per = width // cols
    base = pl.program_id(0) * block_rows

    for h in range(parts):

        @pl.loop(0, tiles)
        def _(f):
            for j in range(per):
                at = pl.ds(j * cols, cols)
                right = jnp.concatenate(
                    [pieces[h * groups + t][f, :, at] for t in range(groups)], axis=0
                )
                place = pl.multiple_of((f * parts + h) * width + j * cols, cols)
                dense[:, pl.ds(place, cols)] = (
                    jnp.dot(x_ref[...], right, preferred_element_type=jnp.float32) * scale
                )

    lane = lax.broadcasted_iota(jnp.int32, (BS, 2 * BS), 1)

    @pl.loop(0, block_rows)
    def _(i):
        rows = pl.ds(pl.multiple_of(i * BS, BS), BS)
        for q in range(kept // (2 * BS)):
            low, high = idx[base + i, 2 * q], idx[base + i, 2 * q + 1]
            a = dense[rows, pl.ds(pl.multiple_of((low // 2) * (2 * BS), 2 * BS), 2 * BS)]
            b = dense[rows, pl.ds(pl.multiple_of((high // 2) * (2 * BS), 2 * BS), 2 * BS)]
            a = pltpu.roll(a, (low % 2) * BS, 1)
            b = pltpu.roll(b, ((high + 1) % 2) * BS, 1)
            o_ref[i, :, q * 2 * BS : (q + 1) * 2 * BS] = jnp.where(lane < BS, a, b)


def weight_gradient(col_idx, features_t, cotangents):
    rows, tokens = features_t.shape
    kept = col_idx.shape[1] * BS
    block_rows = min(4, rows // BS)
    flat = [piece for half in cotangents for piece in half]
    return pl.pallas_call(
        functools.partial(grad_kernel, float(tokens) ** -0.5, len(cotangents)),
        out_shape=jax.ShapeDtypeStruct((rows // BS, BS, kept), jnp.float32),
        grid_spec=pltpu.PrefetchScalarGridSpec(
            num_scalar_prefetch=1,
            grid=(rows // BS // block_rows,),
            in_specs=[pl.BlockSpec((block_rows * BS, tokens), lambda i, idx: (i, 0))]
            + [
                pl.BlockSpec(
                    flat[0].shape, lambda i, idx: (0, 0, 0), pipeline_mode=pl.Buffered(1)
                )
            ]
            * len(flat),
            out_specs=pl.BlockSpec((block_rows, BS, kept), lambda i, idx: (i, 0, 0)),
            scratch_shapes=[pltpu.VMEM((block_rows * BS, FF), jnp.float32)],
        ),
        compiler_params=pltpu.CompilerParams(vmem_limit_bytes=VMEM),
        cost_estimate=pl.CostEstimate(
            flops=2 * tokens * rows * FF,
            bytes_accessed=2 * tokens * FF + 4 * rows * kept,
            transcendentals=0,
        ),
    )(col_idx, features_t, *flat)


def shift(x, axis, by):
    size = lax.axis_size(axis)
    return lax.ppermute(x, axis, [(i, (i + by) % size) for i in range(size)])


def exchange(x):
    pieces = [x] + [shift(x, "dp", d) for d in range(1, lax.axis_size("dp"))]
    others = [shift(p, "sub", d) for d in range(1, lax.axis_size("sub")) for p in pieces]
    return pieces + others


def body(features, values, col_idx, cotangent):
    tiles = lax.axis_size("fsdp")
    rows = values.shape[0] * BS
    half = cotangent.shape[1] // 2
    halves = [
        lax.all_gather(cotangent[:, h * half : (h + 1) * half], "fsdp", axis=0) for h in range(2)
    ]
    all_features = jnp.concatenate(exchange(features), axis=0)
    weight_t = expand(col_idx, values.reshape(rows, -1).T)
    own = lax.axis_index("fsdp").astype(jnp.int32).reshape(1)
    partial = project(own, features, weight_t, tiles)
    total = partial[0].astype(jnp.float32)
    for d in range(1, tiles):
        total = total + shift(partial[d], "fsdp", d).astype(jnp.float32)
    projected = total.astype(jnp.bfloat16)
    input_grad = back(halves, weight_t)
    weight_grad = weight_gradient(col_idx, all_features.T, [exchange(h) for h in halves])
    return (projected, input_grad, weight_grad)


def solution(mesh):
    in_specs = (
        P(("rep", "dp", "sub"), "fsdp"),
        P("fsdp", None, None),
        P("fsdp", None),
        P(("rep", "dp", "sub"), "fsdp"),
    )
    out_specs = (
        P(("rep", "dp", "sub"), "fsdp"),
        P(("rep", "dp", "sub"), "fsdp"),
        P(("rep", "fsdp"), None, None),
    )
    return jax.shard_map(body, mesh=mesh, in_specs=in_specs, out_specs=out_specs, check_vma=False)
```

```python
import functools

import jax
import jax.numpy as jnp
from jax import lax
from jax.experimental import pallas as pl
from jax.experimental.pallas import tpu as pltpu
from jax.sharding import PartitionSpec as P

BS = 64
NBC = 256
FF = BS * NBC
VMEM = 60 * 1024 * 1024
PARTS = 4


def expand_kernel(idx, vt_ref, w_ref):
    pair = pl.program_id(0)
    keep = vt_ref.shape[0] // BS
    chunk = 512

    @pl.loop(0, FF // chunk)
    def _(i):
        w_ref[pl.ds(pl.multiple_of(i * chunk, chunk), chunk), :] = jnp.zeros(
            (chunk, 2 * BS), w_ref.dtype
        )

    lane = lax.broadcasted_iota(jnp.int32, (BS, 2 * BS), 1)
    for half in range(2):
        mask = (lane >= BS) if half else (lane < BS)

        @pl.loop(0, keep, unroll=4)
        def _(k):
            place = pl.ds(pl.multiple_of(idx[2 * pair + half, k] * BS, BS), BS)
            block = vt_ref[pl.ds(pl.multiple_of(k * BS, BS), BS), :]
            w_ref[place, :] = jnp.where(mask, block, w_ref[place, :])


def expand(col_idx, values_t):
    depth, rows = values_t.shape
    return pl.pallas_call(
        expand_kernel,
        out_shape=jax.ShapeDtypeStruct((FF, rows), values_t.dtype),
        grid_spec=pltpu.PrefetchScalarGridSpec(
            num_scalar_prefetch=1,
            grid=(rows // (2 * BS),),
            in_specs=[pl.BlockSpec((depth, 2 * BS), lambda i, idx: (0, i))],
            out_specs=pl.BlockSpec((FF, 2 * BS), lambda i, idx: (0, i)),
        ),
        compiler_params=pltpu.CompilerParams(vmem_limit_bytes=VMEM),
        cost_estimate=pl.CostEstimate(
            flops=0, bytes_accessed=2 * rows * (FF + depth), transcendentals=0
        ),
    )(col_idx, values_t)


def project_kernel(x_ref, w_ref, o_ref):
    o_ref[0] = lax.dot_general(
        x_ref[...], w_ref[...], (((1,), (1,)), ((), ())), preferred_element_type=jnp.float32
    ).astype(o_ref.dtype)


def project(features, weight_t, tiles):
    tokens, rows = features.shape
    width = FF // tiles
    cols = min(2048, width)
    per = width // cols
    return pl.pallas_call(
        project_kernel,
        out_shape=jax.ShapeDtypeStruct((tiles, tokens, width), jnp.bfloat16),
        grid=(tiles, per),
        in_specs=[
            pl.BlockSpec((tokens, rows), lambda f, j: (0, 0)),
            pl.BlockSpec((cols, rows), lambda f, j: (f * per + j, 0)),
        ],
        out_specs=pl.BlockSpec((1, tokens, cols), lambda f, j: (f, 0, j)),
        compiler_params=pltpu.CompilerParams(vmem_limit_bytes=VMEM),
        cost_estimate=pl.CostEstimate(
            flops=2 * tokens * rows * FF, bytes_accessed=2 * FF * (rows + tokens), transcendentals=0
        ),
    )(features, weight_t)


def back_kernel(parts, *refs):
    w_ref, o_ref, total = refs[parts:]
    f = pl.program_id(0)

    @pl.when(f == 0)
    def _():
        total[...] = jnp.zeros_like(total)

    for h in range(parts):
        cols = refs[h].shape[2]
        total[...] += jnp.dot(
            refs[h][0], w_ref[h * cols : (h + 1) * cols, :], preferred_element_type=jnp.float32
        )

    @pl.when(f == pl.num_programs(0) - 1)
    def _():
        o_ref[...] = total[...].astype(o_ref.dtype)


def back(cotangents, weight_t):
    parts = len(cotangents)
    tiles, tokens, cols = cotangents[0].shape
    rows = weight_t.shape[1]
    return pl.pallas_call(
        functools.partial(back_kernel, parts),
        out_shape=jax.ShapeDtypeStruct((tokens, rows), jnp.bfloat16),
        grid=(tiles,),
        in_specs=[pl.BlockSpec((1, tokens, cols), lambda f: (f, 0, 0))] * parts
        + [pl.BlockSpec((parts * cols, rows), lambda f: (f, 0))],
        out_specs=pl.BlockSpec((tokens, rows), lambda f: (0, 0)),
        scratch_shapes=[pltpu.VMEM((tokens, rows), jnp.float32)],
        compiler_params=pltpu.CompilerParams(vmem_limit_bytes=VMEM),
        cost_estimate=pl.CostEstimate(
            flops=2 * tokens * rows * FF, bytes_accessed=2 * FF * (rows + tokens), transcendentals=0
        ),
    )(*cotangents, weight_t)


def grad_kernel(scale, parts, idx, x_ref, *refs):
    o_ref, dense = refs[-2:]
    pieces = refs[:-2]
    groups = len(pieces) // parts
    tiles, part, width = pieces[0].shape
    block_rows, _, kept = o_ref.shape
    cols = min(512, width)
    per = width // cols
    base = pl.program_id(0) * block_rows

    for h in range(parts):

        @pl.loop(0, tiles)
        def _(f):
            for j in range(per):
                at = pl.ds(j * cols, cols)
                right = jnp.concatenate(
                    [pieces[h * groups + t][f, :, at] for t in range(groups)], axis=0
                )
                place = pl.multiple_of((f * parts + h) * width + j * cols, cols)
                dense[:, pl.ds(place, cols)] = (
                    jnp.dot(x_ref[...], right, preferred_element_type=jnp.float32) * scale
                )

    lane = lax.broadcasted_iota(jnp.int32, (BS, 2 * BS), 1)

    @pl.loop(0, block_rows)
    def _(i):
        rows = pl.ds(pl.multiple_of(i * BS, BS), BS)
        for q in range(kept // (2 * BS)):
            low, high = idx[base + i, 2 * q], idx[base + i, 2 * q + 1]
            a = dense[rows, pl.ds(pl.multiple_of((low // 2) * (2 * BS), 2 * BS), 2 * BS)]
            b = dense[rows, pl.ds(pl.multiple_of((high // 2) * (2 * BS), 2 * BS), 2 * BS)]
            a = pltpu.roll(a, (low % 2) * BS, 1)
            b = pltpu.roll(b, ((high + 1) % 2) * BS, 1)
            o_ref[i, :, q * 2 * BS : (q + 1) * 2 * BS] = jnp.where(lane < BS, a, b)


def weight_gradient(col_idx, features_t, cotangents):
    rows, tokens = features_t.shape
    kept = col_idx.shape[1] * BS
    block_rows = min(4, rows // BS)
    flat = [piece for half in cotangents for piece in half]
    return pl.pallas_call(
        functools.partial(grad_kernel, float(tokens) ** -0.5, len(cotangents)),
        out_shape=jax.ShapeDtypeStruct((rows // BS, BS, kept), jnp.float32),
        grid_spec=pltpu.PrefetchScalarGridSpec(
            num_scalar_prefetch=1,
            grid=(rows // BS // block_rows,),
            in_specs=[pl.BlockSpec((block_rows * BS, tokens), lambda i, idx: (i, 0))]
            + [
                pl.BlockSpec(
                    flat[0].shape, lambda i, idx: (0, 0, 0), pipeline_mode=pl.Buffered(1)
                )
            ]
            * len(flat),
            out_specs=pl.BlockSpec((block_rows, BS, kept), lambda i, idx: (i, 0, 0)),
            scratch_shapes=[pltpu.VMEM((block_rows * BS, FF), jnp.float32)],
        ),
        compiler_params=pltpu.CompilerParams(vmem_limit_bytes=VMEM),
        cost_estimate=pl.CostEstimate(
            flops=2 * tokens * rows * FF,
            bytes_accessed=2 * tokens * FF + 4 * rows * kept,
            transcendentals=0,
        ),
    )(col_idx, features_t, *flat)


def shift(x, axis, by):
    size = lax.axis_size(axis)
    return lax.ppermute(x, axis, [(i, (i + by) % size) for i in range(size)])


def exchange(x):
    pieces = [x] + [shift(x, "dp", d) for d in range(1, lax.axis_size("dp"))]
    others = [shift(p, "sub", d) for d in range(1, lax.axis_size("sub")) for p in pieces]
    return pieces + others


def body(features, values, col_idx, cotangent):
    tiles = lax.axis_size("fsdp")
    rows = values.shape[0] * BS
    width = cotangent.shape[1] // PARTS
    pieces = [
        lax.all_gather(cotangent[:, h * width : (h + 1) * width], "fsdp", axis=0)
        for h in range(PARTS)
    ]
    all_features = jnp.concatenate(exchange(features), axis=0)
    weight_t = expand(col_idx, values.reshape(rows, -1).T)
    partial = project(features, weight_t, tiles)
    partial, pieces[1] = lax.optimization_barrier((partial, pieces[1]))
    projected = lax.psum_scatter(partial, "fsdp", scatter_dimension=0)
    input_grad = back(pieces, weight_t)
    exchanged = [exchange(p) for p in pieces]
    weight_grad = weight_gradient(col_idx, all_features.T, exchanged)
    return (projected, input_grad, weight_grad)


def solution(mesh):
    in_specs = (
        P(("rep", "dp", "sub"), "fsdp"),
        P("fsdp", None, None),
        P("fsdp", None),
        P(("rep", "dp", "sub"), "fsdp"),
    )
    out_specs = (
        P(("rep", "dp", "sub"), "fsdp"),
        P(("rep", "dp", "sub"), "fsdp"),
        P(("rep", "fsdp"), None, None),
    )
    return jax.shard_map(body, mesh=mesh, in_specs=in_specs, out_specs=out_specs, check_vma=False)
```

```python
import functools

import jax
import jax.numpy as jnp
from jax import lax
from jax.experimental import pallas as pl
from jax.experimental.pallas import tpu as pltpu
from jax.sharding import PartitionSpec as P

BS = 64
NBC = 256
FF = BS * NBC
VMEM = 60 * 1024 * 1024
PARTS = (2, 1, 1)


def expand_kernel(idx, vt_ref, w_ref):
    pair = pl.program_id(0)
    keep = vt_ref.shape[0] // BS
    chunk = 512

    @pl.loop(0, FF // chunk)
    def _(i):
        w_ref[pl.ds(pl.multiple_of(i * chunk, chunk), chunk), :] = jnp.zeros(
            (chunk, 2 * BS), w_ref.dtype
        )

    lane = lax.broadcasted_iota(jnp.int32, (BS, 2 * BS), 1)
    for half in range(2):
        mask = (lane >= BS) if half else (lane < BS)

        @pl.loop(0, keep, unroll=4)
        def _(k):
            place = pl.ds(pl.multiple_of(idx[2 * pair + half, k] * BS, BS), BS)
            block = vt_ref[pl.ds(pl.multiple_of(k * BS, BS), BS), :]
            w_ref[place, :] = jnp.where(mask, block, w_ref[place, :])


def expand(col_idx, values_t):
    depth, rows = values_t.shape
    return pl.pallas_call(
        expand_kernel,
        out_shape=jax.ShapeDtypeStruct((FF, rows), values_t.dtype),
        grid_spec=pltpu.PrefetchScalarGridSpec(
            num_scalar_prefetch=1,
            grid=(rows // (2 * BS),),
            in_specs=[pl.BlockSpec((depth, 2 * BS), lambda i, idx: (0, i))],
            out_specs=pl.BlockSpec((FF, 2 * BS), lambda i, idx: (0, i)),
        ),
        compiler_params=pltpu.CompilerParams(vmem_limit_bytes=VMEM),
        cost_estimate=pl.CostEstimate(
            flops=0, bytes_accessed=2 * rows * (FF + depth), transcendentals=0
        ),
    )(col_idx, values_t)


def project_kernel(x_ref, w_ref, o_ref):
    o_ref[0] = lax.dot_general(
        x_ref[...], w_ref[...], (((1,), (1,)), ((), ())), preferred_element_type=jnp.float32
    ).astype(o_ref.dtype)


def project(features, weight_t, tiles):
    tokens, rows = features.shape
    width = FF // tiles
    cols = min(2048, width)
    per = width // cols
    return pl.pallas_call(
        project_kernel,
        out_shape=jax.ShapeDtypeStruct((tiles, tokens, width), jnp.bfloat16),
        grid=(tiles, per),
        in_specs=[
            pl.BlockSpec((tokens, rows), lambda f, j: (0, 0)),
            pl.BlockSpec((cols, rows), lambda f, j: (f * per + j, 0)),
        ],
        out_specs=pl.BlockSpec((1, tokens, cols), lambda f, j: (f, 0, j)),
        compiler_params=pltpu.CompilerParams(vmem_limit_bytes=VMEM),
        cost_estimate=pl.CostEstimate(
            flops=2 * tokens * rows * FF, bytes_accessed=2 * FF * (rows + tokens), transcendentals=0
        ),
    )(features, weight_t)


def back_kernel(parts, *refs):
    w_ref, o_ref, total = refs[parts:]
    f = pl.program_id(0)

    @pl.when(f == 0)
    def _():
        total[...] = jnp.zeros_like(total)

    start = 0
    for h in range(parts):
        cols = refs[h].shape[2]
        total[...] += jnp.dot(
            refs[h][0], w_ref[start : start + cols, :], preferred_element_type=jnp.float32
        )
        start += cols

    @pl.when(f == pl.num_programs(0) - 1)
    def _():
        o_ref[...] = total[...].astype(o_ref.dtype)


def back(cotangents, weight_t):
    parts = len(cotangents)
    tiles, tokens, _ = cotangents[0].shape
    rows = weight_t.shape[1]
    return pl.pallas_call(
        functools.partial(back_kernel, parts),
        out_shape=jax.ShapeDtypeStruct((tokens, rows), jnp.bfloat16),
        grid=(tiles,),
        in_specs=[pl.BlockSpec((1, tokens, c.shape[2]), lambda f: (f, 0, 0)) for c in cotangents]
        + [pl.BlockSpec((FF // tiles, rows), lambda f: (f, 0))],
        out_specs=pl.BlockSpec((tokens, rows), lambda f: (0, 0)),
        scratch_shapes=[pltpu.VMEM((tokens, rows), jnp.float32)],
        compiler_params=pltpu.CompilerParams(vmem_limit_bytes=VMEM),
        cost_estimate=pl.CostEstimate(
            flops=2 * tokens * rows * FF, bytes_accessed=2 * FF * (rows + tokens), transcendentals=0
        ),
    )(*cotangents, weight_t)


def grad_kernel(scale, parts, idx, x_ref, *refs):
    o_ref, dense = refs[-2:]
    pieces = refs[:-2]
    groups = len(pieces) // parts
    tiles = pieces[0].shape[0]
    block_rows, _, kept = o_ref.shape
    base = pl.program_id(0) * block_rows
    start = 0

    for h in range(parts):
        width = pieces[h * groups].shape[2]
        cols = min(512, width)

        @pl.loop(0, tiles)
        def _(f, h=h, width=width, cols=cols, start=start):
            for j in range(width // cols):
                at = pl.ds(j * cols, cols)
                right = jnp.concatenate(
                    [pieces[h * groups + t][f, :, at] for t in range(groups)], axis=0
                )
                place = pl.multiple_of(f * (FF // tiles) + start + j * cols, 128)
                dense[:, pl.ds(place, cols)] = (
                    jnp.dot(x_ref[...], right, preferred_element_type=jnp.float32) * scale
                )

        start += width

    lane = lax.broadcasted_iota(jnp.int32, (BS, 2 * BS), 1)

    @pl.loop(0, block_rows)
    def _(i):
        rows = pl.ds(pl.multiple_of(i * BS, BS), BS)
        for q in range(kept // (2 * BS)):
            low, high = idx[base + i, 2 * q], idx[base + i, 2 * q + 1]
            a = dense[rows, pl.ds(pl.multiple_of((low // 2) * (2 * BS), 2 * BS), 2 * BS)]
            b = dense[rows, pl.ds(pl.multiple_of((high // 2) * (2 * BS), 2 * BS), 2 * BS)]
            a = pltpu.roll(a, (low % 2) * BS, 1)
            b = pltpu.roll(b, ((high + 1) % 2) * BS, 1)
            o_ref[i, :, q * 2 * BS : (q + 1) * 2 * BS] = jnp.where(lane < BS, a, b)


def weight_gradient(col_idx, features_t, cotangents):
    rows, tokens = features_t.shape
    kept = col_idx.shape[1] * BS
    block_rows = min(4, rows // BS)
    flat = [piece for half in cotangents for piece in half]
    return pl.pallas_call(
        functools.partial(grad_kernel, float(tokens) ** -0.5, len(cotangents)),
        out_shape=jax.ShapeDtypeStruct((rows // BS, BS, kept), jnp.float32),
        grid_spec=pltpu.PrefetchScalarGridSpec(
            num_scalar_prefetch=1,
            grid=(rows // BS // block_rows,),
            in_specs=[pl.BlockSpec((block_rows * BS, tokens), lambda i, idx: (i, 0))]
            + [
                pl.BlockSpec(piece.shape, lambda i, idx: (0, 0, 0), pipeline_mode=pl.Buffered(1))
                for piece in flat
            ],
            out_specs=pl.BlockSpec((block_rows, BS, kept), lambda i, idx: (i, 0, 0)),
            scratch_shapes=[pltpu.VMEM((block_rows * BS, FF), jnp.float32)],
        ),
        compiler_params=pltpu.CompilerParams(vmem_limit_bytes=VMEM),
        cost_estimate=pl.CostEstimate(
            flops=2 * tokens * rows * FF,
            bytes_accessed=2 * tokens * FF + 4 * rows * kept,
            transcendentals=0,
        ),
    )(col_idx, features_t, *flat)


def shift(x, axis, by):
    size = lax.axis_size(axis)
    return lax.ppermute(x, axis, [(i, (i + by) % size) for i in range(size)])


def along_dp(x):
    return [x] + [shift(x, "dp", d) for d in range(1, lax.axis_size("dp"))]


def along_sub(pieces):
    return pieces + [
        shift(p, "sub", d) for d in range(1, lax.axis_size("sub")) for p in pieces
    ]


def body(features, values, col_idx, cotangent):
    tiles = lax.axis_size("fsdp")
    rows = values.shape[0] * BS
    unit = cotangent.shape[1] // sum(PARTS)
    pieces, start = [], 0
    for share in PARTS:
        part = cotangent[:, start * unit : (start + share) * unit]
        pieces.append(lax.all_gather(part, "fsdp", axis=0))
        start += share
    all_features = jnp.concatenate(along_sub(along_dp(features)), axis=0).T
    values_t = values.reshape(rows, -1).T
    values_t, all_features = lax.optimization_barrier((values_t, all_features))
    weight_t = expand(col_idx, values_t)
    partial = project(features, weight_t, tiles)
    partial, pieces[0] = lax.optimization_barrier((partial, pieces[0]))
    projected = lax.psum_scatter(partial, "fsdp", scatter_dimension=0)
    columns = []
    for h in range(len(PARTS)):
        if h:
            columns[-1], pieces[h] = lax.optimization_barrier((columns[-1], pieces[h]))
        columns.append(along_dp(pieces[h]))
    input_grad = back(pieces, weight_t)
    columns[-1], input_grad = lax.optimization_barrier((columns[-1], input_grad))
    weight_grad = weight_gradient(col_idx, all_features, [along_sub(c) for c in columns])
    return (projected, input_grad, weight_grad)


def solution(mesh):
    in_specs = (
        P(("rep", "dp", "sub"), "fsdp"),
        P("fsdp", None, None),
        P("fsdp", None),
        P(("rep", "dp", "sub"), "fsdp"),
    )
    out_specs = (
        P(("rep", "dp", "sub"), "fsdp"),
        P(("rep", "dp", "sub"), "fsdp"),
        P(("rep", "fsdp"), None, None),
    )
    return jax.shard_map(body, mesh=mesh, in_specs=in_specs, out_specs=out_specs, check_vma=False)
```

```python
import functools

import jax
import jax.numpy as jnp
from jax import lax
from jax.experimental import pallas as pl
from jax.experimental.pallas import tpu as pltpu
from jax.sharding import PartitionSpec as P

BS = 64
NBC = 256
FF = BS * NBC
VMEM = 60 * 1024 * 1024
PARTS = (2, 1, 1)


def expand_kernel(idx, vt_ref, w_ref):
    pair = pl.program_id(0)
    keep = vt_ref.shape[0] // BS
    chunk = 512

    @pl.loop(0, FF // chunk)
    def _(i):
        w_ref[pl.ds(pl.multiple_of(i * chunk, chunk), chunk), :] = jnp.zeros(
            (chunk, 2 * BS), w_ref.dtype
        )

    lane = lax.broadcasted_iota(jnp.int32, (BS, 2 * BS), 1)
    for half in range(2):
        mask = (lane >= BS) if half else (lane < BS)

        @pl.loop(0, keep, unroll=4)
        def _(k):
            place = pl.ds(pl.multiple_of(idx[2 * pair + half, k] * BS, BS), BS)
            block = vt_ref[pl.ds(pl.multiple_of(k * BS, BS), BS), :]
            w_ref[place, :] = jnp.where(mask, block, w_ref[place, :])


def expand(col_idx, values_t):
    depth, rows = values_t.shape
    return pl.pallas_call(
        expand_kernel,
        out_shape=jax.ShapeDtypeStruct((FF, rows), values_t.dtype),
        grid_spec=pltpu.PrefetchScalarGridSpec(
            num_scalar_prefetch=1,
            grid=(rows // (2 * BS),),
            in_specs=[pl.BlockSpec((depth, 2 * BS), lambda i, idx: (0, i))],
            out_specs=pl.BlockSpec((FF, 2 * BS), lambda i, idx: (0, i)),
        ),
        compiler_params=pltpu.CompilerParams(vmem_limit_bytes=VMEM),
        cost_estimate=pl.CostEstimate(
            flops=0, bytes_accessed=2 * rows * (FF + depth), transcendentals=0
        ),
    )(col_idx, values_t)


def project_kernel(x_ref, w_ref, o_ref):
    o_ref[0] = lax.dot_general(
        x_ref[...], w_ref[...], (((1,), (1,)), ((), ())), preferred_element_type=jnp.float32
    ).astype(o_ref.dtype)


def project(features, weight_t, tiles):
    tokens, rows = features.shape
    width = FF // tiles
    cols = min(2048, width)
    per = width // cols
    return pl.pallas_call(
        project_kernel,
        out_shape=jax.ShapeDtypeStruct((tiles, tokens, width), jnp.bfloat16),
        grid=(tiles, per),
        in_specs=[
            pl.BlockSpec((tokens, rows), lambda f, j: (0, 0)),
            pl.BlockSpec((cols, rows), lambda f, j: (f * per + j, 0)),
        ],
        out_specs=pl.BlockSpec((1, tokens, cols), lambda f, j: (f, 0, j)),
        compiler_params=pltpu.CompilerParams(vmem_limit_bytes=VMEM),
        cost_estimate=pl.CostEstimate(
            flops=2 * tokens * rows * FF, bytes_accessed=2 * FF * (rows + tokens), transcendentals=0
        ),
    )(features, weight_t)


def back_kernel(parts, *refs):
    w_ref, o_ref, total = refs[parts:]
    f = pl.program_id(0)

    @pl.when(f == 0)
    def _():
        total[...] = jnp.zeros_like(total)

    start = 0
    for h in range(parts):
        cols = refs[h].shape[2]
        total[...] += jnp.dot(
            refs[h][0], w_ref[start : start + cols, :], preferred_element_type=jnp.float32
        )
        start += cols

    @pl.when(f == pl.num_programs(0) - 1)
    def _():
        o_ref[...] = total[...].astype(o_ref.dtype)


def back(cotangents, weight_t):
    parts = len(cotangents)
    tiles, tokens, _ = cotangents[0].shape
    rows = weight_t.shape[1]
    return pl.pallas_call(
        functools.partial(back_kernel, parts),
        out_shape=jax.ShapeDtypeStruct((tokens, rows), jnp.bfloat16),
        grid=(tiles,),
        in_specs=[pl.BlockSpec((1, tokens, c.shape[2]), lambda f: (f, 0, 0)) for c in cotangents]
        + [pl.BlockSpec((FF // tiles, rows), lambda f: (f, 0))],
        out_specs=pl.BlockSpec((tokens, rows), lambda f: (0, 0)),
        scratch_shapes=[pltpu.VMEM((tokens, rows), jnp.float32)],
        compiler_params=pltpu.CompilerParams(vmem_limit_bytes=VMEM),
        cost_estimate=pl.CostEstimate(
            flops=2 * tokens * rows * FF, bytes_accessed=2 * FF * (rows + tokens), transcendentals=0
        ),
    )(*cotangents, weight_t)


def grad_kernel(scale, parts, idx, x_ref, *refs):
    o_ref, dense = refs[-2:]
    pieces = refs[:-2]
    groups = len(pieces) // parts
    tiles = pieces[0].shape[0]
    block_rows, _, kept = o_ref.shape
    base = pl.program_id(0) * block_rows
    start = 0

    for h in range(parts):
        width = pieces[h * groups].shape[2]
        cols = min(512, width)

        @pl.loop(0, tiles)
        def _(f, h=h, width=width, cols=cols, start=start):
            for j in range(width // cols):
                at = pl.ds(j * cols, cols)
                right = jnp.concatenate(
                    [pieces[h * groups + t][f, :, at] for t in range(groups)], axis=0
                )
                place = pl.multiple_of(f * (FF // tiles) + start + j * cols, 128)
                dense[:, pl.ds(place, cols)] = (
                    jnp.dot(x_ref[...], right, preferred_element_type=jnp.float32) * scale
                )

        start += width

    lane = lax.broadcasted_iota(jnp.int32, (BS, 2 * BS), 1)

    @pl.loop(0, block_rows)
    def _(i):
        rows = pl.ds(pl.multiple_of(i * BS, BS), BS)
        for q in range(kept // (2 * BS)):
            low, high = idx[base + i, 2 * q], idx[base + i, 2 * q + 1]
            a = dense[rows, pl.ds(pl.multiple_of((low // 2) * (2 * BS), 2 * BS), 2 * BS)]
            b = dense[rows, pl.ds(pl.multiple_of((high // 2) * (2 * BS), 2 * BS), 2 * BS)]
            a = pltpu.roll(a, (low % 2) * BS, 1)
            b = pltpu.roll(b, ((high + 1) % 2) * BS, 1)
            o_ref[i, :, q * 2 * BS : (q + 1) * 2 * BS] = jnp.where(lane < BS, a, b)


def weight_gradient(col_idx, features_t, cotangents):
    rows, tokens = features_t.shape
    kept = col_idx.shape[1] * BS
    block_rows = min(4, rows // BS)
    flat = [piece for half in cotangents for piece in half]
    return pl.pallas_call(
        functools.partial(grad_kernel, float(tokens) ** -0.5, len(cotangents)),
        out_shape=jax.ShapeDtypeStruct((rows // BS, BS, kept), jnp.float32),
        grid_spec=pltpu.PrefetchScalarGridSpec(
            num_scalar_prefetch=1,
            grid=(rows // BS // block_rows,),
            in_specs=[pl.BlockSpec((block_rows * BS, tokens), lambda i, idx: (i, 0))]
            + [
                pl.BlockSpec(piece.shape, lambda i, idx: (0, 0, 0), pipeline_mode=pl.Buffered(1))
                for piece in flat
            ],
            out_specs=pl.BlockSpec((block_rows, BS, kept), lambda i, idx: (i, 0, 0)),
            scratch_shapes=[pltpu.VMEM((block_rows * BS, FF), jnp.float32)],
        ),
        compiler_params=pltpu.CompilerParams(vmem_limit_bytes=VMEM),
        cost_estimate=pl.CostEstimate(
            flops=2 * tokens * rows * FF,
            bytes_accessed=2 * tokens * FF + 4 * rows * kept,
            transcendentals=0,
        ),
    )(col_idx, features_t, *flat)


def shift(x, axis, by):
    size = lax.axis_size(axis)
    return lax.ppermute(x, axis, [(i, (i + by) % size) for i in range(size)])


def along_dp(x):
    return [x] + [shift(x, "dp", d) for d in range(1, lax.axis_size("dp"))]


def along_sub(pieces):
    return pieces + [
        shift(p, "sub", d) for d in range(1, lax.axis_size("sub")) for p in pieces
    ]


def body(features, values, col_idx, cotangent):
    tiles = lax.axis_size("fsdp")
    rows = values.shape[0] * BS
    unit = cotangent.shape[1] // sum(PARTS)
    pieces, start = [], 0
    for share in PARTS:
        part = cotangent[:, start * unit : (start + share) * unit]
        pieces.append(lax.all_gather(part, "fsdp", axis=0))
        start += share
    all_features = jnp.concatenate(along_sub(along_dp(features)), axis=0).T
    values_t = values.reshape(rows, -1).T
    values_t, all_features = lax.optimization_barrier((values_t, all_features))
    weight_t = expand(col_idx, values_t)
    weight_t, pieces[0] = lax.optimization_barrier((weight_t, pieces[0]))
    columns = [along_dp(pieces[0])]
    columns[0], pieces[1], weight_t = lax.optimization_barrier((columns[0], pieces[1], weight_t))
    partial = project(features, weight_t, tiles)
    projected = lax.psum_scatter(partial, "fsdp", scatter_dimension=0)
    for h in range(1, len(PARTS)):
        columns.append(along_dp(pieces[h]))
        if h + 1 < len(PARTS):
            columns[h], pieces[h + 1], partial = lax.optimization_barrier(
                (columns[h], pieces[h + 1], partial)
            )
    input_grad = back(pieces, weight_t)
    columns[-1], input_grad = lax.optimization_barrier((columns[-1], input_grad))
    weight_grad = weight_gradient(col_idx, all_features, [along_sub(c) for c in columns])
    return (projected, input_grad, weight_grad)


def solution(mesh):
    in_specs = (
        P(("rep", "dp", "sub"), "fsdp"),
        P("fsdp", None, None),
        P("fsdp", None),
        P(("rep", "dp", "sub"), "fsdp"),
    )
    out_specs = (
        P(("rep", "dp", "sub"), "fsdp"),
        P(("rep", "dp", "sub"), "fsdp"),
        P(("rep", "fsdp"), None, None),
    )
    return jax.shard_map(body, mesh=mesh, in_specs=in_specs, out_specs=out_specs, check_vma=False)
```
